128 devices in a mesh: clip: 64 (over z, y, x_hi, core), seq: 2 (over x_lo).
Axes of the slice: x: 4 (x_hi: 2, x_lo: 2; x = x_hi * 2 + x_lo), y: 4, z: 4, core: 2. Of those that a mesh axis runs over, the one named last changes fastest.
Arguments:
- query_space: bfloat16 [256, 704, 1536], P(('clip', 'seq')), may hold values from -36 to 36
- key_space: bfloat16 [256, 704, 1536], P(('clip', 'seq')), may hold values from -6 to 6
- value_space: bfloat16 [256, 704, 1536], P(('clip', 'seq')), may hold values from -6 to 6
- query_time: bfloat16 [256, 704, 1536], P(('clip', 'seq')), may hold values from -36 to 36
- key_time: bfloat16 [256, 704, 1536], P(('clip', 'seq')), may hold values from -6 to 6
- frame_counts: int32 [16], replicated, may hold values from 8 to 16, as said below
- heights: int32 [16], replicated, may hold values from 11 to 22, as said below
- widths: int32 [16], replicated, may hold values from 16 to 32, as said below
Outputs:
- time_out: bfloat16 [256, 704, 1536], P(('clip', 'seq'))
The draws below stay inside these ranges and needn't reach their ends.
Inputs may be any that keep to these rules, and one draw needn't show every extreme that they name: The first frame_counts[c] frame slots of clip c are live; some clip has all 16. `heights`: some clip has all 22 rows. `widths`: some clip has all 32 columns.
All inputs are finite; a program needn't handle non-finite values.
Results may differ from the reference program's by a relative error of at most 0.015.
Values may be sent and summed in bfloat16 or wider, within the bound.
No kernel may reach another device: no remote copies, remote signals or barrier semaphores. Data moves between devices by JAX's collectives and lax.ppermute only.
A program may use at most 192 MiB of HBM per device.

```python
import jax
import jax.numpy as jnp
from jax import lax

HEADS = 12
HEAD = 128
HD = 1536
HMAX = 22
WMAX = 32
PMAX = 704
FMAX = 16
CLIPS = 16
FRAMES = 256


def draw_query_space(key, part):
    key = jax.random.fold_in(key, 11)
    return jax.random.truncated_normal(key, -6.0, 6.0, (FRAMES, PMAX, HD), jnp.float32).astype(jnp.bfloat16)


def draw_key_space(key, part):
    key = jax.random.fold_in(key, 12)
    return jax.random.truncated_normal(key, -6.0, 6.0, (FRAMES, PMAX, HD), jnp.float32).astype(jnp.bfloat16)


def draw_query_time(key, part):
    key = jax.random.fold_in(key, 13)
    return jax.random.truncated_normal(key, -6.0, 6.0, (FRAMES, PMAX, HD), jnp.float32).astype(jnp.bfloat16)


def draw_key_time(key, part):
    key = jax.random.fold_in(key, 14)
    return jax.random.truncated_normal(key, -6.0, 6.0, (FRAMES, PMAX, HD), jnp.float32).astype(jnp.bfloat16)


def bounded_counts(key, largest):
    counts = jax.random.randint(key, (CLIPS,), largest - largest // 2, largest + 1)
    fullest = jax.random.randint(jax.random.fold_in(key, 2), (), 0, CLIPS)
    return jnp.where(jnp.arange(CLIPS) == fullest, largest, counts).astype(jnp.int32)


def draw_frame_counts(key, part):
    key = jax.random.fold_in(key, 21)
    return bounded_counts(key, FMAX)


def draw_heights(key, part):
    key = jax.random.fold_in(key, 22)
    return bounded_counts(key, HMAX)


def draw_widths(key, part):
    key = jax.random.fold_in(key, 23)
    return bounded_counts(key, WMAX)


def steps_of(own_key, shape, cuts, low, high):
    def one(axis_at, parts):
        draws = jax.random.uniform(jax.random.fold_in(jax.random.fold_in(own_key, 6), axis_at), (parts,), jnp.float32, low / len(cuts), high / len(cuts))
        return jnp.repeat(jnp.exp(draws), shape[axis_at] // parts).reshape((-1,) + (1,) * (len(shape) - axis_at - 1))

    gain = one(*cuts[0])
    for cut in cuts[1:]:
        gain = gain * one(*cut)
    return gain


def gaussian(rng, shape, deviation, bound, pieces=(), kind=jnp.bfloat16):
    values = jax.random.normal(rng, shape, jnp.float32) * deviation
    if len(pieces) > 0:
        values = steps_of(rng, shape, pieces, -0.22, 0.18) * values
    return jnp.clip(values, min=-bound, max=bound).astype(kind)


def setup_inputs(seed: int = 0) -> dict:
    streams_of = jax.random.split(jax.random.key(seed), 9)
    query_space = draw_query_space(jax.random.fold_in(streams_of[8], 71), 0)
    key_space = draw_key_space(jax.random.fold_in(streams_of[8], 71), 0)
    value_space = gaussian(streams_of[2], (FRAMES, PMAX, HD), 1.0, 6.0, ((0, 128),))
    query_time = draw_query_time(jax.random.fold_in(streams_of[8], 71), 0)
    key_time = draw_key_time(jax.random.fold_in(streams_of[8], 71), 0)
    frame_counts = draw_frame_counts(jax.random.fold_in(streams_of[8], 71), 0)
    heights = draw_heights(jax.random.fold_in(streams_of[8], 71), 0)
    widths = draw_widths(jax.random.fold_in(streams_of[8], 71), 0)
    return dict(query_space=query_space, key_space=key_space, value_space=value_space, query_time=query_time, key_time=key_time, frame_counts=frame_counts, heights=heights, widths=widths)


def live_slots(slots, height, width):
    return (slots // WMAX < height) & (slots % WMAX < width)


def soft_weights(scores, key_live):
    scores = jnp.where(key_live, scores, -jnp.inf)
    top = jnp.max(scores, axis=-1, keepdims=True)
    expo = jnp.exp(scores - top)
    total = jnp.sum(expo, axis=-1, keepdims=True)
    return (expo / total).astype(jnp.bfloat16)


def reference(query_space, key_space, value_space, query_time, key_time, frame_counts, heights, widths):
    scale = HEAD ** -0.5
    slots = jnp.arange(PMAX, dtype=jnp.int32)
    rows = jnp.arange(FRAMES, dtype=jnp.int32)
    clip_of = (rows // FMAX).astype(jnp.int32)
    frame_of = (rows % FMAX).astype(jnp.int32)

    def space_frame(item):
        queries, keys, values, clip_id, frame_id = item
        token_live = live_slots(slots, heights[clip_id], widths[clip_id])
        frame_live = frame_id < frame_counts[clip_id]
        query_heads = queries.astype(jnp.float32).reshape(PMAX, HEADS, HEAD)
        key_heads = keys.astype(jnp.float32).reshape(PMAX, HEADS, HEAD)
        value_heads = values.astype(jnp.float32).reshape(PMAX, HEADS, HEAD)
        scores = jnp.einsum("phd,khd->hpk", query_heads, key_heads) * scale
        weights = soft_weights(scores, token_live[None, None, :])
        mixed = jnp.einsum("hpk,khd->phd", weights.astype(jnp.float32), value_heads)
        keep = (token_live & frame_live)[:, None, None]
        return jnp.where(keep, mixed, 0.0).reshape(PMAX, HD).astype(jnp.bfloat16)

    space_out = lax.map(space_frame, (query_space, key_space, value_space, clip_of, frame_of))

    def time_clip(item):
        queries, keys, values, clip_id = item
        token_live = live_slots(slots, heights[clip_id], widths[clip_id])
        frame_live = jnp.arange(FMAX, dtype=jnp.int32) < frame_counts[clip_id]
        query_heads = queries.astype(jnp.float32).reshape(FMAX, PMAX, HEADS, HEAD)
        key_heads = keys.astype(jnp.float32).reshape(FMAX, PMAX, HEADS, HEAD)
        value_heads = values.astype(jnp.float32).reshape(FMAX, PMAX, HEADS, HEAD)
        scores = jnp.einsum("fshd,gshd->shfg", query_heads, key_heads) * scale
        weights = soft_weights(scores, frame_live[None, None, None, :])
        mixed = jnp.einsum("shfg,gshd->fshd", weights.astype(jnp.float32), value_heads)
        keep = (frame_live[:, None] & token_live[None, :])[:, :, None, None]
        return jnp.where(keep, mixed, 0.0).reshape(FMAX, PMAX, HD).astype(jnp.bfloat16)

    clip_ids = jnp.arange(CLIPS, dtype=jnp.int32)
    time_out = lax.map(time_clip, (query_time.reshape(CLIPS, FMAX, PMAX, HD),
                                   key_time.reshape(CLIPS, FMAX, PMAX, HD),
                                   space_out.reshape(CLIPS, FMAX, PMAX, HD), clip_ids))
    return time_out.reshape(FRAMES, PMAX, HD)
```

```python
from functools import partial

import jax
import jax.numpy as jnp
from jax import lax
from jax.experimental import pallas as pl
from jax.experimental.pallas import tpu as pltpu
from jax.sharding import PartitionSpec as P

HEAD = 128
WMAX = 32
HMAX = 22
ROW = 8
CHIPS = 4
PER = 3
SIDE = 4
ROWS = SIDE * SIDE
AXES = ("clip", "seq")
SLOTS = HMAX * WMAX
FEATURES = CHIPS * PER * HEAD
GAIN = HEAD**-0.5 * 1.4426950408889634
LOW = -1e30
UNIT = 16
BLOCKS = SLOTS // UNIT
MOST = 6
SPARE = MOST * UNIT
SWEEPS = 4
ALONE = 10
REST = 20
MORE = 8
MAIN = ((0, ALONE // 2), (ALONE, REST // 2))
FURTHER = ((0, MORE // 2),)
TURNS = ((0, 2), (2, 1))
PACK = 64
REACH = 160
VMEM_LIMIT = 56 * 1024 * 1024

ME, WIDTH, COUNT, FRAMES, HEIGHT, KEPT, START = range(7)
GIVEN, GIVEN_AT, TAKEN, TAKEN_AT, HOST_AT = 8, 12, 16, 20, 24
FRAMES_OF = 32
TABLE = 128

SMEM = pl.BlockSpec(memory_space=pltpu.SMEM)
ANYWHERE = pl.BlockSpec(memory_space=pl.ANY)


def params():
    return pltpu.CompilerParams(vmem_limit_bytes=VMEM_LIMIT)


def cost(flops, megabytes, transcendentals=0):
    return pl.CostEstimate(flops=flops, bytes_accessed=megabytes * 2**20, transcendentals=transcendentals)


def half(*shape):
    return jax.ShapeDtypeStruct(shape, jnp.bfloat16)


def dot(left, right, transposed=False):
    dims = (((1,), (1 if transposed else 0,)), ((), ()))
    return lax.dot_general(left, right, dims, preferred_element_type=jnp.float32)


def lines(block):
    return pl.multiple_of(block * UNIT, UNIT)


def neighbour(row, way):
    z, y = row // SIDE, row % SIDE
    step = 1 if way % 2 == 0 else SIDE - 1
    if way < 2:
        return (z + step) % SIDE * SIDE + y
    return z * SIDE + (y + step) % SIDE


def plan_kernel(place, counts, heights, widths, table, passes, load, flow):
    me, mine = place[0] % ROW, place[0] // ROW

    def blocks(row):
        return (heights[row] * widths[row] + UNIT - 1) // UNIT

    for row in range(ROWS):
        load[row] = blocks(row)
        flow[0, row] = 0
        flow[1, row] = 0
    for sweep in range(SWEEPS):
        for axis in range(2):
            for row in range(ROWS):
                gap = load[row] - load[neighbour(row, 2 * axis)]
                share = jnp.where(gap > 0, 1, -1) * ((jnp.abs(gap) + 1) // 5)
                flow[axis, row] = jnp.clip(flow[axis, row] + share, -MOST, MOST)
        for row in range(ROWS):
            total = blocks(row)
            for axis in range(2):
                total = total - flow[axis, row] + flow[axis, neighbour(row, 2 * axis + 1)]
            load[row] = total

    def edges_of(row):
        return [
            flow[0, row],
            -flow[0, neighbour(row, 1)],
            flow[1, row],
            -flow[1, neighbour(row, 3)],
        ]

    least = jnp.int32(BLOCKS)
    for row in range(ROWS):
        least = jnp.minimum(least, blocks(row) - sum(jnp.maximum(edge, 0) for edge in edges_of(row)))

    @pl.when(least < ALONE)
    def _():
        for row in range(ROWS):
            load[row] = blocks(row)
            flow[0, row] = 0
            flow[1, row] = 0

    largest = jnp.int32(0)
    for row in range(ROWS):
        largest = jnp.maximum(largest, load[row])
    passes[0] = jnp.maximum(largest - ALONE - REST + MORE - 1, 0) // MORE

    def list_of(row):
        edges = edges_of(row)
        kept = blocks(row) - sum(jnp.maximum(edge, 0) for edge in edges)
        given = [jnp.maximum(edges[way], 0) for way in range(4)]
        taken = [jnp.maximum(-edges[way ^ 1], 0) for way in range(4)]
        given_at, taken_at = [kept], [kept]
        for way in range(3):
            given_at.append(given_at[way] + given[way])
            taken_at.append(taken_at[way] + taken[way])
        return kept, given, given_at, taken, taken_at

    kept, given, given_at, taken, taken_at = list_of(mine)
    table[ME] = me
    table[WIDTH] = widths[mine]
    table[COUNT] = heights[mine] * widths[mine]
    table[FRAMES] = counts[mine]
    table[HEIGHT] = heights[mine]
    table[KEPT] = kept
    table[START] = 0
    for way in range(4):
        table[GIVEN + way] = given[way]
        table[GIVEN_AT + way] = given_at[way]
        table[TAKEN + way] = taken[way]
        table[TAKEN_AT + way] = taken_at[way]
        table[HOST_AT + way] = list_of(neighbour(mine, way))[4][way]

    def fill(slot, carry):
        table[FRAMES_OF + slot] = counts[mine]
        return carry

    lax.fori_loop(0, BLOCKS + MOST, fill, 0)
    for way in range(4):
        giver = neighbour(mine, way ^ 1)

        def mark(slot, carry):
            table[FRAMES_OF + slot] = counts[giver]
            return carry

        lax.fori_loop(taken_at[way], taken_at[way] + taken[way], mark, 0)


def make_plan(place, counts, heights, widths):
    return pl.pallas_call(
        plan_kernel,
        in_specs=[SMEM] * 4,
        out_specs=[SMEM] * 2,
        out_shape=[jax.ShapeDtypeStruct((TABLE,), jnp.int32), jax.ShapeDtypeStruct((1,), jnp.int32)],
        scratch_shapes=[pltpu.SMEM((ROWS,), jnp.int32), pltpu.SMEM((2, ROWS), jnp.int32)],
        cost_estimate=cost(1000, 0),
        name="plan",
    )(place, counts, heights, widths)


def gather_matrix(start, width, count):
    row = lax.div(start, width)
    base = jnp.minimum(row * WMAX, SLOTS - REACH)
    at = start + lax.broadcasted_iota(jnp.int32, (PACK, REACH), 0)
    line = jnp.full((PACK, REACH), row, jnp.int32)
    for step in range(1, 5):
        line = line + jnp.where(at >= (row + step) * width, 1, 0)
    slot = at + line * (WMAX - width) - base
    slot = jnp.where(at < count, slot, -1)
    picked = lax.broadcasted_iota(jnp.int32, (PACK, REACH), 1) == slot
    return jnp.where(picked, 1.0, 0.0).astype(jnp.bfloat16)


def reach_of(start, width):
    return pl.multiple_of(jnp.minimum(lax.div(start, width) * WMAX, SLOTS - REACH), WMAX)


def chip_and_core(place):
    return (place >> 2) * 2 + (place & 1), (place >> 1) & 1


def all_of(copies):
    for copy in copies:
        copy.start()
    for copy in copies:
        copy.wait()


def pack_kernel(info, queries, keys, own, alone, *refs):
    gifts, (picks, loaded, packed, in_sems, own_sems, alone_sems, gift_sems) = refs[:4], refs[4:]
    width, count = info[WIDTH], info[COUNT]
    loads = [
        pltpu.make_async_copy((queries, keys)[i // 2].at[i % 2], loaded.at[i], in_sems.at[i]) for i in range(4)
    ]
    for copy in loads:
        copy.start()
    for index in range(SLOTS // PACK):
        picks[index] = gather_matrix(index * PACK, width, count)
    packed[:, SLOTS:, :] = jnp.zeros((4, SPARE, FEATURES), jnp.bfloat16)
    copies = []
    rows = ALONE * UNIT // 2
    for i in range(4):
        loads[i].wait()
        for index in range(SLOTS // PACK):
            window = loaded[i, pl.ds(reach_of(index * PACK, width), REACH), :]
            packed[i, pl.ds(index * PACK, PACK), :] = dot(picks[index], window).astype(jnp.bfloat16)
        mine = [pltpu.make_async_copy(packed.at[i], own.at[i], own_sems.at[i])]
        for way in range(4):
            part = packed.at[i, pl.ds(lines(info[GIVEN_AT + way]), SPARE)]
            mine.append(pltpu.make_async_copy(part, gifts[way].at[i], gift_sems.at[i, way]))
        for place in range(ROW):
            chip, core = chip_and_core(place)
            part = packed.at[i, pl.ds(core * rows, rows), pl.ds(chip * PER * HEAD, PER * HEAD)]
            mine.append(pltpu.make_async_copy(part, alone.at[place, i], alone_sems.at[i, place]))
        for copy in mine:
            copy.start()
        copies += mine
    for copy in copies:
        copy.wait()


def pack(info, queries, keys):
    own, alone, *gifts = pl.pallas_call(
        pack_kernel,
        in_specs=[SMEM, ANYWHERE, ANYWHERE],
        out_specs=[ANYWHERE] * 6,
        out_shape=[half(4, SLOTS + SPARE, FEATURES), half(ROW, 4, ALONE * UNIT // 2, PER * HEAD)]
        + [half(4, SPARE, FEATURES)] * 4,
        scratch_shapes=[
            pltpu.VMEM((SLOTS // PACK, PACK, REACH), jnp.bfloat16),
            pltpu.VMEM((4, SLOTS, FEATURES), jnp.bfloat16),
            pltpu.VMEM((4, SLOTS + SPARE, FEATURES), jnp.bfloat16),
            pltpu.SemaphoreType.DMA((4,)),
            pltpu.SemaphoreType.DMA((4,)),
            pltpu.SemaphoreType.DMA((4, ROW)),
            pltpu.SemaphoreType.DMA((4, 4)),
        ],
        compiler_params=params(),
        cost_estimate=cost(0, 40),
        name="pack",
    )(info, queries, keys)
    return own, alone, gifts


def merge_kernel(parts, info, own, *refs):
    gifts, (out, merged, own_sem, gift_sems, out_sems) = refs[:4], refs[4:]
    columns = out.shape[3]
    first = parts[0][0]
    start = info[START] + first
    size = merged.shape[1] // UNIT
    copy = pltpu.make_async_copy(own.at[:, pl.ds(lines(start), size * UNIT)], merged, own_sem)
    copy.start()
    copy.wait()

    def each(act):
        for way in range(4):
            for block in range(MOST):
                at = info[TAKEN_AT + way] + block - start

                @pl.when((block < info[TAKEN + way]) & (at >= 0) & (at < size))
                def _():
                    part = gifts[way].at[:, pl.ds(block * UNIT, UNIT)]
                    to = merged.at[:, pl.ds(lines(at), UNIT)]
                    act(pltpu.make_async_copy(part, to, gift_sems.at[way, block]))

    each(lambda copy: copy.start())
    each(lambda copy: copy.wait())
    copies = []
    for place in range(ROW):
        chip, core = chip_and_core(place)
        done = 0
        for index, (at, each_core) in enumerate(parts):
            rows = each_core * UNIT
            part = merged.at[:, pl.ds((at - first) * UNIT + core * rows, rows), pl.ds(chip * columns, columns)]
            to = out.at[place, :, pl.ds(done, rows)]
            copies.append(pltpu.make_async_copy(part, to, out_sems.at[place, index]))
            done += rows
    all_of(copies)


def merge(info, own, gifts, parts):
    count, _, features = own.shape
    rows = sum(each for _, each in parts) * UNIT
    return pl.pallas_call(
        partial(merge_kernel, parts),
        in_specs=[SMEM] + [ANYWHERE] * 5,
        out_specs=ANYWHERE,
        out_shape=half(ROW, count, rows, features // CHIPS),
        scratch_shapes=[
            pltpu.VMEM((count, 2 * rows, features), jnp.bfloat16),
            pltpu.SemaphoreType.DMA,
            pltpu.SemaphoreType.DMA((4, MOST)),
            pltpu.SemaphoreType.DMA((ROW, 2)),
        ],
        compiler_params=params(),
        cost_estimate=cost(0, max(1, 6 * count * features // FEATURES)),
        name="merge",
    )(info, own, *gifts)


QBLOCK = 176


def space_kernel(number, info, q_ref, k_ref, v_ref, own, *refs):
    gifts, (picks, qc, kc, vc, made, own_sem, gift_sems) = refs[:4], refs[4:]
    frame, which = pl.program_id(0), pl.program_id(1)
    me, width, count = info[ME], info[WIDTH], info[COUNT]
    alive = me * 2 + frame < info[FRAMES]
    column = pl.ds(pl.multiple_of(which * HEAD, HEAD), HEAD)

    @pl.when((frame == 0) & (which == 0))
    def _():
        vc[:, HEAD:] = jnp.ones((SLOTS, HEAD), jnp.bfloat16)
        made[:, SLOTS:, :] = jnp.zeros((2, SPARE, CHIPS * number * HEAD), jnp.bfloat16)
        for index in range(SLOTS // PACK):
            picks[index] = gather_matrix(index * PACK, width, count)

    @pl.when(alive)
    def _():
        for index in range(SLOTS // PACK):
            at = pl.ds(reach_of(index * PACK, width), REACH)
            to = pl.ds(index * PACK, PACK)
            window = jnp.concatenate([q_ref[0, at, :], k_ref[0, at, :], v_ref[0, at, :]], axis=1)
            found = dot(picks[index], window).astype(jnp.bfloat16)
            qc[to, :] = found[:, :HEAD]
            kc[to, :] = found[:, HEAD : 2 * HEAD]
            vc[to, :HEAD] = found[:, 2 * HEAD :]

    bias = jnp.where(lax.broadcasted_iota(jnp.int32, (1, SLOTS), 1) < count, 0.0, LOW)
    for part in range(2):
        busy = alive & (part * 2 * QBLOCK < count)

        @pl.when(busy)
        def _():
            for block in range(part * 2, part * 2 + 2):
                to = pl.ds(block * QBLOCK, QBLOCK)
                scores = dot(qc[to, :], kc[...], True) + bias
                top = jnp.max(scores, axis=-1, keepdims=True)
                expo = jnp.exp2((scores - top) * GAIN).astype(jnp.bfloat16)
                mixed = dot(expo, vc[...])
                made[frame, to, column] = (mixed[:, :HEAD] / mixed[:, HEAD:]).astype(jnp.bfloat16)

        @pl.when(jnp.logical_not(busy))
        def _():
            made[frame, pl.ds(part * 2 * QBLOCK, 2 * QBLOCK), column] = jnp.zeros((2 * QBLOCK, HEAD), jnp.bfloat16)

    @pl.when((frame == 1) & (which == CHIPS * number - 1))
    def _():
        copies = [pltpu.make_async_copy(made, own, own_sem)]
        for way in range(4):
            part = made.at[:, pl.ds(lines(info[GIVEN_AT + way]), SPARE)]
            copies.append(pltpu.make_async_copy(part, gifts[way], gift_sems.at[way]))
        all_of(copies)


def space(info, queries, keys, values, turn):
    first, number = turn
    features = CHIPS * number * HEAD
    spec = pl.BlockSpec((1, SLOTS, HEAD), lambda f, i: (f, 0, i // number * PER + first + i % number))
    steps = 2 * CHIPS * number
    own, *gifts = pl.pallas_call(
        partial(space_kernel, number),
        grid=(2, CHIPS * number),
        in_specs=[SMEM, spec, spec, spec],
        out_specs=[ANYWHERE] * 5,
        out_shape=[half(2, SLOTS + SPARE, features)] + [half(2, SPARE, features)] * 4,
        scratch_shapes=[
            pltpu.VMEM((SLOTS // PACK, PACK, REACH), jnp.bfloat16),
            pltpu.VMEM((SLOTS, HEAD), jnp.bfloat16),
            pltpu.VMEM((SLOTS, HEAD), jnp.bfloat16),
            pltpu.VMEM((SLOTS, 2 * HEAD), jnp.bfloat16),
            pltpu.VMEM((2, SLOTS + SPARE, features), jnp.bfloat16),
            pltpu.SemaphoreType.DMA,
            pltpu.SemaphoreType.DMA((4,)),
        ],
        compiler_params=params(),
        cost_estimate=cost(steps * 8 * SLOTS * SLOTS * HEAD, number * 8, steps * SLOTS * SLOTS),
        name="space",
    )(info, queries, keys, values)
    return own, gifts


def time_kernel(parts, info, *refs):
    turned, (vs, outs) = refs[: len(parts)], refs[len(parts) :]
    core = (info[ME] >> 1) & 1
    span = ROW * 2 * UNIT
    down = lax.broadcasted_iota(jnp.int32, (span, span), 0)
    along = lax.broadcasted_iota(jnp.int32, (span, span), 1)
    frame = jnp.where((down & 15) == (along & 15), along >> 4, span)
    ones = jnp.ones((span, HEAD), jnp.bfloat16)
    done = 0
    for (at, each_core), ref in zip(parts, turned):
        first = info[START] + at + core * each_core

        def step(index, carry, ref=ref, first=first, done=done):
            here = pl.ds(lines(index), UNIT)
            there = pl.ds(lines(index + done), UNIT)
            seen = frame < info[FRAMES_OF + first + index]
            queries = ref[:, 0:2, here, :].reshape(span, HEAD)
            keys = ref[:, 2:4, here, :].reshape(span, HEAD)
            values = vs[:, :, there, :].reshape(span, HEAD)
            scores = jnp.where(seen, dot(queries, keys, True), LOW)
            top = jnp.max(scores, axis=-1, keepdims=True)
            expo = jnp.exp2((scores - top) * GAIN).astype(jnp.bfloat16)
            mixed = dot(expo, jnp.concatenate([values, ones], axis=1))
            made = (mixed[:, :HEAD] / mixed[:, HEAD:]).astype(jnp.bfloat16)
            outs[:, :, there, :] = made.reshape(ROW, 2, UNIT, HEAD)
            return carry

        lax.fori_loop(0, each_core, step, 0, unroll=5 if each_core % 5 == 0 else 1)
        done += each_core


def time_attention(info, turned, values, turn, parts):
    first, number = turn
    rows = values.shape[2]
    wide = [pl.BlockSpec((ROW, 4, each * UNIT, HEAD), lambda h: (0, 0, 0, first + h)) for _, each in parts]
    thin = pl.BlockSpec((ROW, 2, rows, HEAD), lambda h: (0, 0, 0, h))
    return pl.pallas_call(
        partial(time_kernel, parts),
        grid=(number,),
        in_specs=[SMEM, *wide, thin],
        out_specs=thin,
        out_shape=half(ROW, 2, rows, number * HEAD),
        compiler_params=params(),
        cost_estimate=cost(number * rows * 16 * 256 * 128 * 4, number * 5, number * rows * 16 * 256),
        name="time",
    )(info, *turned, values)


def divide_kernel(parts, info, pieces, own, *refs):
    gifts, (merged, in_sems, own_sem, gift_sems) = refs[:4], refs[4:]
    columns = pieces.shape[3]
    size = merged.shape[1] // UNIT
    start = info[START]
    copies = []
    for place in range(ROW):
        chip, core = chip_and_core(place)
        done = 0
        for index, (at, each_core) in enumerate(parts):
            rows = each_core * UNIT
            part = merged.at[:, pl.ds(at * UNIT + core * rows, rows), pl.ds(chip * columns, columns)]
            copies.append(
                pltpu.make_async_copy(pieces.at[place, :, pl.ds(done, rows)], part, in_sems.at[place, index])
            )
            done += rows
    all_of(copies)
    copy = pltpu.make_async_copy(merged, own, own_sem)
    copy.start()

    def each(act):
        for way in range(4):
            for block in range(MOST):
                at = info[TAKEN_AT + way] + block - start

                @pl.when((block < info[TAKEN + way]) & (at >= 0) & (at < size))
                def _():
                    part = merged.at[:, pl.ds(lines(at), UNIT)]
                    to = gifts[way].at[:, pl.ds(block * UNIT, UNIT)]
                    act(pltpu.make_async_copy(part, to, gift_sems.at[way, block]))

    each(lambda copy: copy.start())
    each(lambda copy: copy.wait())
    copy.wait()


def divide(info, pieces, parts):
    features = CHIPS * pieces.shape[3]
    size = 2 * sum(each for _, each in parts)
    own, *gifts = pl.pallas_call(
        partial(divide_kernel, parts),
        in_specs=[SMEM, ANYWHERE],
        out_specs=[ANYWHERE] * 5,
        out_shape=[half(2, size * UNIT, features)] + [half(2, SPARE, features)] * 4,
        scratch_shapes=[
            pltpu.VMEM((2, size * UNIT, features), jnp.bfloat16),
            pltpu.SemaphoreType.DMA((ROW, 2)),
            pltpu.SemaphoreType.DMA,
            pltpu.SemaphoreType.DMA((4, MOST)),
        ],
        compiler_params=params(),
        cost_estimate=cost(0, max(1, 8 * features // FEATURES)),
        name="divide",
    )(info, pieces)
    return own, gifts


SPREAD = 64
SOURCE = 80


def unpack_kernel(turn, adding, info, own, *refs):
    gifts, (old, out, held, made, own_sems, gift_sems, out_sems) = refs[:4], refs[4:]
    first, number = turn
    me, width, height = info[ME], info[WIDTH], info[HEIGHT]
    start, kept = info[START], info[KEPT]
    size = own.shape[1] // UNIT

    def column(ref, frame, chip):
        return ref.at[frame, :, pl.ds((chip * PER + first) * HEAD, number * HEAD)]

    def place(frame, chip):
        return made.at[frame, :, pl.ds(chip * number * HEAD, number * HEAD)]

    spots = [(frame, chip) for frame in range(2) for chip in range(CHIPS)]
    if adding:
        all_of([pltpu.make_async_copy(column(old, *spot), place(*spot), out_sems.at[spot]) for spot in spots])
        held[...] = jnp.zeros(held.shape, jnp.bfloat16)
    else:
        copy = pltpu.make_async_copy(own, held.at[:, pl.ds(0, size * UNIT)], own_sems.at[0])
        copy.start()
        held[:, size * UNIT :, :] = jnp.zeros((2, held.shape[1] - size * UNIT, held.shape[2]), jnp.bfloat16)
        copy.wait()
        for block in range(size):

            @pl.when(block >= kept)
            def _():
                held[:, pl.ds(block * UNIT, UNIT), :] = jnp.zeros((2, UNIT, held.shape[2]), jnp.bfloat16)

    def each(act):
        if adding:
            for block in range(size):

                @pl.when(start + block < kept)
                def _():
                    part = own.at[:, pl.ds(block * UNIT, UNIT)]
                    act(pltpu.make_async_copy(part, held.at[:, pl.ds(lines(start + block), UNIT)], own_sems.at[block]))

        for way in range(4):
            for block in range(MOST):
                at = info[HOST_AT + way] + block - start

                @pl.when((block < info[GIVEN + way]) & (at >= 0) & (at < size))
                def _():
                    part = gifts[way].at[:, pl.ds(block * UNIT, UNIT)]
                    to = held.at[:, pl.ds(lines(info[GIVEN_AT + way] + block), UNIT)]
                    act(pltpu.make_async_copy(part, to, gift_sems.at[way, block]))

    each(lambda copy: copy.start())
    each(lambda copy: copy.wait())
    for index in range(SLOTS // SPREAD):
        row = index * 2
        from_row = pl.multiple_of((row * width) & -16, 16)
        at = lax.broadcasted_iota(jnp.int32, (SPREAD, SOURCE), 0)
        line = row + (at >> 5)
        wanted = line * width + (at & 31) - from_row
        wanted = jnp.where(((at & 31) < width) & (line < height), wanted, -1)
        picked = lax.broadcasted_iota(jnp.int32, (SPREAD, SOURCE), 1) == wanted
        to = pl.ds(index * SPREAD, SPREAD)
        for frame in range(2):
            alive = me * 2 + frame < info[FRAMES]
            matrix = jnp.where(picked & alive, 1.0, 0.0).astype(jnp.bfloat16)
            value = dot(matrix, held[frame, pl.ds(from_row, SOURCE), :])
            if adding:
                value = value + made[frame, to, :].astype(jnp.float32)
            made[frame, to, :] = value.astype(jnp.bfloat16)
    all_of([pltpu.make_async_copy(place(*spot), column(out, *spot), out_sems.at[spot]) for spot in spots])


def unpack(info, own, gifts, out, turn, adding):
    features = own.shape[2]
    first = out is None

    def body(info, own, *refs):
        refs = list(refs)
        if first:
            refs.insert(4, None)
        unpack_kernel(turn, adding, info, own, *refs)

    return pl.pallas_call(
        body,
        in_specs=[SMEM] + [ANYWHERE] * (5 if first else 6),
        out_specs=ANYWHERE,
        out_shape=half(2, SLOTS, FEATURES),
        input_output_aliases={} if first else {6: 0},
        scratch_shapes=[
            pltpu.VMEM((2, SLOTS + SPARE, features), jnp.bfloat16),
            pltpu.VMEM((2, SLOTS, features), jnp.bfloat16),
            pltpu.SemaphoreType.DMA((MORE,)),
            pltpu.SemaphoreType.DMA((4, MOST)),
            pltpu.SemaphoreType.DMA((2, CHIPS)),
        ],
        compiler_params=params(),
        cost_estimate=cost(0, max(1, 12 * features // FEATURES)),
        name="unpack",
    )(info, own, *gifts, *([] if first else [out]))


def step_along(value, way):
    size = lax.axis_size(AXES)
    return lax.ppermute(value, AXES, [(i, neighbour(i // ROW, way) * ROW + i % ROW) for i in range(size)])


def give(gifts):
    return [step_along(gifts[way], way) for way in range(4)]


def give_back(gifts):
    return [step_along(gifts[way], way ^ 1) for way in range(4)]


def exchange(pieces):
    size = lax.axis_size(AXES)
    groups = [list(range(i, i + ROW)) for i in range(0, size, ROW)]
    return lax.all_to_all(pieces, AXES, 0, 0, axis_index_groups=groups, tiled=True)


def after(value, *others):
    return lax.optimization_barrier((value, *others))[0]


def local(query_space, key_space, value_space, query_time, key_time, frame_counts, heights, widths):
    place = lax.axis_index(AXES).astype(jnp.int32).reshape(1)
    info, passes = make_plan(place, frame_counts, heights, widths)
    own, alone, gifts = pack(info, query_time, key_time)
    head = exchange(alone)
    gifts = give(gifts)
    spaced = []
    late = after(info, own)
    for index, turn in enumerate(TURNS):
        made, sent = space(late, query_space, key_space, value_space, turn)
        spaced.append((made, give(sent)))
        if index == 0:
            pieces = merge(info, own, after(gifts, made), MAIN[1:])
            late = after(info, pieces)
            tail = exchange(after(pieces, head))
    turned = (head, tail)
    previous = tail
    values = []
    for index, (made, sent) in enumerate(spaced):
        if index + 1 < len(spaced):
            sent = after(sent, spaced[index + 1][0])
        previous = exchange(after(merge(info, made, sent, MAIN), previous))
        values.append(previous)
    out = None
    for index, turn in enumerate(TURNS):
        made = time_attention(info, turned, values[index], turn, MAIN)
        previous = exchange(after(made, previous))
        mine, back = divide(info, previous if out is None else after(previous, out), MAIN)
        out = unpack(info, mine, give_back(back), out, turn, False)

    def further(index, out):
        here = info.at[START].set(ALONE + REST + index * MORE)
        turned = (exchange(merge(here, own, gifts, FURTHER)),)
        for (made, sent), turn in zip(spaced, TURNS):
            values = exchange(merge(here, made, sent, FURTHER))
            back = exchange(time_attention(here, turned, values, turn, FURTHER))
            mine, back = divide(here, back, FURTHER)
            out = unpack(here, mine, give_back(back), out, turn, True)
        return out

    return lax.fori_loop(0, passes[0], further, out)


def solution(mesh):
    split = P(AXES, None, None)
    return jax.shard_map(
        local,
        mesh=mesh,
        in_specs=(split,) * 5 + (P(),) * 3,
        out_specs=split,
        check_vma=False,
    )
```

```python
from functools import partial

import jax
import jax.numpy as jnp
from jax import lax
from jax.experimental import pallas as pl
from jax.experimental.pallas import tpu as pltpu
from jax.sharding import PartitionSpec as P

HEAD = 128
WMAX = 32
HMAX = 22
ROW = 8
CHIPS = 4
PER = 3
SIDE = 4
ROWS = SIDE * SIDE
AXES = ("clip", "seq")
SLOTS = HMAX * WMAX
FEATURES = CHIPS * PER * HEAD
GAIN = HEAD**-0.5 * 1.4426950408889634
LOW = -1e30
UNIT = 16
BLOCKS = SLOTS // UNIT
MOST = 6
SPARE = MOST * UNIT
DIVISORS = (4, 2, 2)
ALONE = 10
REST = 20
MORE = 8
MAIN = ((0, ALONE // 2), (ALONE, REST // 2))
FURTHER = ((0, MORE // 2),)
TURNS = ((0, 1), (1, 2))
PACK = 64
REACH = 160
VMEM_LIMIT = 56 * 1024 * 1024

ME, WIDTH, COUNT, FRAMES, HEIGHT, KEPT, START = range(7)
GIVEN, GIVEN_AT, TAKEN, TAKEN_AT, HOST_AT = 8, 12, 16, 20, 24
FRAMES_OF = 32
TABLE = 128

SMEM = pl.BlockSpec(memory_space=pltpu.SMEM)
ANYWHERE = pl.BlockSpec(memory_space=pl.ANY)


def params():
    return pltpu.CompilerParams(vmem_limit_bytes=VMEM_LIMIT)


def cost(flops, megabytes, transcendentals=0):
    return pl.CostEstimate(flops=flops, bytes_accessed=megabytes * 2**20, transcendentals=transcendentals)


def half(*shape):
    return jax.ShapeDtypeStruct(shape, jnp.bfloat16)


def dot(left, right, transposed=False):
    dims = (((1,), (1 if transposed else 0,)), ((), ()))
    return lax.dot_general(left, right, dims, preferred_element_type=jnp.float32)


def lines(block):
    return pl.multiple_of(block * UNIT, UNIT)


def neighbour(row, way):
    z, y = row // SIDE, row % SIDE
    step = 1 if way % 2 == 0 else SIDE - 1
    if way < 2:
        return (z + step) % SIDE * SIDE + y
    return z * SIDE + (y + step) % SIDE


def plan_kernel(place, counts, heights, widths, table, passes, load, flow):
    me, mine = place[0] % ROW, place[0] // ROW

    def blocks(row):
        return (heights[row] * widths[row] + UNIT - 1) // UNIT

    for row in range(ROWS):
        load[row] = blocks(row)
        flow[0, row] = 0
        flow[1, row] = 0
    for divisor in DIVISORS:
        for axis in range(2):
            for row in range(ROWS):
                other = neighbour(row, 2 * axis)
                gap = load[row] - load[other]
                share = jnp.where(gap > 0, 1, -1) * lax.div(jnp.abs(gap), divisor)
                old = flow[axis, row]
                new = jnp.clip(old + share, -MOST, MOST)
                flow[axis, row] = new
                load[row] = load[row] - (new - old)
                load[other] = load[other] + (new - old)

    def edges_of(row):
        return [
            flow[0, row],
            -flow[0, neighbour(row, 1)],
            flow[1, row],
            -flow[1, neighbour(row, 3)],
        ]

    least = jnp.int32(BLOCKS)
    for row in range(ROWS):
        least = jnp.minimum(least, blocks(row) - sum(jnp.maximum(edge, 0) for edge in edges_of(row)))

    @pl.when(least < ALONE)
    def _():
        for row in range(ROWS):
            load[row] = blocks(row)
            flow[0, row] = 0
            flow[1, row] = 0

    largest = jnp.int32(0)
    for row in range(ROWS):
        largest = jnp.maximum(largest, load[row])
    passes[0] = jnp.maximum(largest - ALONE - REST + MORE - 1, 0) // MORE

    def list_of(row):
        edges = edges_of(row)
        kept = blocks(row) - sum(jnp.maximum(edge, 0) for edge in edges)
        given = [jnp.maximum(edges[way], 0) for way in range(4)]
        taken = [jnp.maximum(-edges[way ^ 1], 0) for way in range(4)]
        given_at, taken_at = [kept], [kept]
        for way in range(3):
            given_at.append(given_at[way] + given[way])
            taken_at.append(taken_at[way] + taken[way])
        return kept, given, given_at, taken, taken_at

    kept, given, given_at, taken, taken_at = list_of(mine)
    table[ME] = me
    table[WIDTH] = widths[mine]
    table[COUNT] = heights[mine] * widths[mine]
    table[FRAMES] = counts[mine]
    table[HEIGHT] = heights[mine]
    table[KEPT] = kept
    table[START] = 0
    for way in range(4):
        table[GIVEN + way] = given[way]
        table[GIVEN_AT + way] = given_at[way]
        table[TAKEN + way] = taken[way]
        table[TAKEN_AT + way] = taken_at[way]
        table[HOST_AT + way] = list_of(neighbour(mine, way))[4][way]

    def fill(slot, carry):
        table[FRAMES_OF + slot] = counts[mine]
        return carry

    lax.fori_loop(0, BLOCKS + MOST, fill, 0)
    for way in range(4):
        giver = neighbour(mine, way ^ 1)

        def mark(slot, carry):
            table[FRAMES_OF + slot] = counts[giver]
            return carry

        lax.fori_loop(taken_at[way], taken_at[way] + taken[way], mark, 0)


def make_plan(place, counts, heights, widths):
    return pl.pallas_call(
        plan_kernel,
        in_specs=[SMEM] * 4,
        out_specs=[SMEM] * 2,
        out_shape=[jax.ShapeDtypeStruct((TABLE,), jnp.int32), jax.ShapeDtypeStruct((1,), jnp.int32)],
        scratch_shapes=[pltpu.SMEM((ROWS,), jnp.int32), pltpu.SMEM((2, ROWS), jnp.int32)],
        cost_estimate=cost(1000, 0),
        name="plan",
    )(place, counts, heights, widths)


def gather_matrix(start, width, count):
    row = lax.div(start, width)
    base = jnp.minimum(row * WMAX, SLOTS - REACH)
    at = start + lax.broadcasted_iota(jnp.int32, (PACK, REACH), 0)
    line = jnp.full((PACK, REACH), row, jnp.int32)
    for step in range(1, 5):
        line = line + jnp.where(at >= (row + step) * width, 1, 0)
    slot = at + line * (WMAX - width) - base
    slot = jnp.where(at < count, slot, -1)
    picked = lax.broadcasted_iota(jnp.int32, (PACK, REACH), 1) == slot
    return jnp.where(picked, 1.0, 0.0).astype(jnp.bfloat16)


def reach_of(start, width):
    return pl.multiple_of(jnp.minimum(lax.div(start, width) * WMAX, SLOTS - REACH), WMAX)


def chip_and_core(place):
    return (place >> 2) * 2 + (place & 1), (place >> 1) & 1


def all_of(copies):
    for copy in copies:
        copy.start()
    for copy in copies:
        copy.wait()


def pack_kernel(info, queries, keys, own, alone, *refs):
    gifts, (picks, loaded, packed, in_sems, own_sems, alone_sems, gift_sems) = refs[:4], refs[4:]
    width, count = info[WIDTH], info[COUNT]
    loads = [
        pltpu.make_async_copy((queries, keys)[i // 2].at[i % 2], loaded.at[i], in_sems.at[i]) for i in range(4)
    ]
    for copy in loads:
        copy.start()
    for index in range(SLOTS // PACK):
        picks[index] = gather_matrix(index * PACK, width, count)
    packed[:, SLOTS:, :] = jnp.zeros((4, SPARE, FEATURES), jnp.bfloat16)
    copies = []
    rows = ALONE * UNIT // 2
    for i in range(4):
        loads[i].wait()
        for index in range(SLOTS // PACK):
            window = loaded[i, pl.ds(reach_of(index * PACK, width), REACH), :]
            packed[i, pl.ds(index * PACK, PACK), :] = dot(picks[index], window).astype(jnp.bfloat16)
        mine = [pltpu.make_async_copy(packed.at[i], own.at[i], own_sems.at[i])]
        for way in range(4):
            part = packed.at[i, pl.ds(lines(info[GIVEN_AT + way]), SPARE)]
            mine.append(pltpu.make_async_copy(part, gifts[way].at[i], gift_sems.at[i, way]))
        for place in range(ROW):
            chip, core = chip_and_core(place)
            part = packed.at[i, pl.ds(core * rows, rows), pl.ds(chip * PER * HEAD, PER * HEAD)]
            mine.append(pltpu.make_async_copy(part, alone.at[place, i], alone_sems.at[i, place]))
        for copy in mine:
            copy.start()
        copies += mine
    for copy in copies:
        copy.wait()


def pack(info, queries, keys):
    own, alone, *gifts = pl.pallas_call(
        pack_kernel,
        in_specs=[SMEM, ANYWHERE, ANYWHERE],
        out_specs=[ANYWHERE] * 6,
        out_shape=[half(4, SLOTS + SPARE, FEATURES), half(ROW, 4, ALONE * UNIT // 2, PER * HEAD)]
        + [half(4, SPARE, FEATURES)] * 4,
        scratch_shapes=[
            pltpu.VMEM((SLOTS // PACK, PACK, REACH), jnp.bfloat16),
            pltpu.VMEM((4, SLOTS, FEATURES), jnp.bfloat16),
            pltpu.VMEM((4, SLOTS + SPARE, FEATURES), jnp.bfloat16),
            pltpu.SemaphoreType.DMA((4,)),
            pltpu.SemaphoreType.DMA((4,)),
            pltpu.SemaphoreType.DMA((4, ROW)),
            pltpu.SemaphoreType.DMA((4, 4)),
        ],
        compiler_params=params(),
        cost_estimate=cost(0, 40),
        name="pack",
    )(info, queries, keys)
    return own, alone, gifts


def merge_kernel(parts, info, own, *refs):
    gifts, (out, merged, own_sem, gift_sems, out_sems) = refs[:4], refs[4:]
    columns = out.shape[3]
    first = parts[0][0]
    start = info[START] + first
    size = merged.shape[1] // UNIT
    copy = pltpu.make_async_copy(own.at[:, pl.ds(lines(start), size * UNIT)], merged, own_sem)
    copy.start()
    copy.wait()

    def each(act):
        for way in range(4):
            for block in range(MOST):
                at = info[TAKEN_AT + way] + block - start

                @pl.when((block < info[TAKEN + way]) & (at >= 0) & (at < size))
                def _():
                    part = gifts[way].at[:, pl.ds(block * UNIT, UNIT)]
                    to = merged.at[:, pl.ds(lines(at), UNIT)]
                    act(pltpu.make_async_copy(part, to, gift_sems.at[way, block]))

    each(lambda copy: copy.start())
    each(lambda copy: copy.wait())
    copies = []
    for place in range(ROW):
        chip, core = chip_and_core(place)
        done = 0
        for index, (at, each_core) in enumerate(parts):
            rows = each_core * UNIT
            part = merged.at[:, pl.ds((at - first) * UNIT + core * rows, rows), pl.ds(chip * columns, columns)]
            to = out.at[place, :, pl.ds(done, rows)]
            copies.append(pltpu.make_async_copy(part, to, out_sems.at[place, index]))
            done += rows
    all_of(copies)


def merge(info, own, gifts, parts):
    count, _, features = own.shape
    rows = sum(each for _, each in parts) * UNIT
    return pl.pallas_call(
        partial(merge_kernel, parts),
        in_specs=[SMEM] + [ANYWHERE] * 5,
        out_specs=ANYWHERE,
        out_shape=half(ROW, count, rows, features // CHIPS),
        scratch_shapes=[
            pltpu.VMEM((count, 2 * rows, features), jnp.bfloat16),
            pltpu.SemaphoreType.DMA,
            pltpu.SemaphoreType.DMA((4, MOST)),
            pltpu.SemaphoreType.DMA((ROW, 2)),
        ],
        compiler_params=params(),
        cost_estimate=cost(0, max(1, 6 * count * features // FEATURES)),
        name="merge",
    )(info, own, *gifts)


QBLOCK = SLOTS // 2


def space_kernel(number, info, q_ref, k_ref, v_ref, own, *refs):
    gifts, (picks, qc, kc, vc, made, own_sem, gift_sems) = refs[:4], refs[4:]
    frame, which = pl.program_id(0), pl.program_id(1)
    me, width, count = info[ME], info[WIDTH], info[COUNT]
    alive = me * 2 + frame < info[FRAMES]
    column = pl.ds(pl.multiple_of(which * HEAD, HEAD), HEAD)

    @pl.when((frame == 0) & (which == 0))
    def _():
        vc[:, HEAD:] = jnp.ones((SLOTS, HEAD), jnp.bfloat16)
        made[:, SLOTS:, :] = jnp.zeros((2, SPARE, CHIPS * number * HEAD), jnp.bfloat16)
        for index in range(SLOTS // PACK):
            picks[index] = gather_matrix(index * PACK, width, count)

    @pl.when(alive)
    def _():
        for index in range(SLOTS // PACK):
            at = pl.ds(reach_of(index * PACK, width), REACH)
            to = pl.ds(index * PACK, PACK)
            window = jnp.concatenate([q_ref[0, at, :], k_ref[0, at, :], v_ref[0, at, :]], axis=1)
            found = dot(picks[index], window).astype(jnp.bfloat16)
            qc[to, :] = found[:, :HEAD]
            kc[to, :] = found[:, HEAD : 2 * HEAD]
            vc[to, :HEAD] = found[:, 2 * HEAD :]

    bias = jnp.where(lax.broadcasted_iota(jnp.int32, (1, SLOTS), 1) < count, 0.0, LOW)

    def attend(block):
        to = pl.ds(block * QBLOCK, QBLOCK)
        scores = dot(qc[to, :], kc[...], True) + bias
        top = jnp.max(scores, axis=-1, keepdims=True)
        expo = jnp.exp2((scores - top) * GAIN).astype(jnp.bfloat16)
        mixed = dot(expo, vc[...])
        made[frame, to, column] = (mixed[:, :HEAD] / mixed[:, HEAD:]).astype(jnp.bfloat16)

    def blank(block):
        made[frame, pl.ds(block * QBLOCK, QBLOCK), column] = jnp.zeros((QBLOCK, HEAD), jnp.bfloat16)

    @pl.when(alive & (count > QBLOCK))
    def _():
        attend(0)
        attend(1)

    @pl.when(alive & (count <= QBLOCK))
    def _():
        attend(0)
        blank(1)

    @pl.when(jnp.logical_not(alive))
    def _():
        blank(0)
        blank(1)

    @pl.when((frame == 1) & (which == CHIPS * number - 1))
    def _():
        copies = [pltpu.make_async_copy(made, own, own_sem)]
        for way in range(4):
            part = made.at[:, pl.ds(lines(info[GIVEN_AT + way]), SPARE)]
            copies.append(pltpu.make_async_copy(part, gifts[way], gift_sems.at[way]))
        all_of(copies)


def space(info, queries, keys, values, turn):
    first, number = turn
    features = CHIPS * number * HEAD
    spec = pl.BlockSpec((1, SLOTS, HEAD), lambda f, i: (f, 0, i // number * PER + first + i % number))
    steps = 2 * CHIPS * number
    own, *gifts = pl.pallas_call(
        partial(space_kernel, number),
        grid=(2, CHIPS * number),
        in_specs=[SMEM, spec, spec, spec],
        out_specs=[ANYWHERE] * 5,
        out_shape=[half(2, SLOTS + SPARE, features)] + [half(2, SPARE, features)] * 4,
        scratch_shapes=[
            pltpu.VMEM((SLOTS // PACK, PACK, REACH), jnp.bfloat16),
            pltpu.VMEM((SLOTS, HEAD), jnp.bfloat16),
            pltpu.VMEM((SLOTS, HEAD), jnp.bfloat16),
            pltpu.VMEM((SLOTS, 2 * HEAD), jnp.bfloat16),
            pltpu.VMEM((2, SLOTS + SPARE, features), jnp.bfloat16),
            pltpu.SemaphoreType.DMA,
            pltpu.SemaphoreType.DMA((4,)),
        ],
        compiler_params=params(),
        cost_estimate=cost(steps * 8 * SLOTS * SLOTS * HEAD, number * 8, steps * SLOTS * SLOTS),
        name="space",
    )(info, queries, keys, values)
    return own, gifts


def time_kernel(at, each_core, info, turned, vs, *refs):
    outs = refs[-1]
    rows = outs.shape[2]
    core = (info[ME] >> 1) & 1
    first = info[START] + at + core * each_core + pl.program_id(1) * (rows // UNIT)
    span = ROW * 2 * UNIT
    down = lax.broadcasted_iota(jnp.int32, (span, span), 0)
    along = lax.broadcasted_iota(jnp.int32, (span, span), 1)
    frame = jnp.where((down & 15) == (along & 15), along >> 4, span)
    ones = jnp.ones((span, HEAD), jnp.bfloat16)
    for index in range(rows // UNIT):
        here = pl.ds(index * UNIT, UNIT)
        seen = frame < info[FRAMES_OF + first + index]
        queries = turned[:, 0:2, here, :].reshape(span, HEAD)
        keys = turned[:, 2:4, here, :].reshape(span, HEAD)
        values = vs[:, :, here, :].reshape(span, HEAD)
        scores = jnp.where(seen, dot(queries, keys, True), LOW)
        top = jnp.max(scores, axis=-1, keepdims=True)
        expo = jnp.exp2((scores - top) * GAIN).astype(jnp.bfloat16)
        mixed = dot(expo, jnp.concatenate([values, ones], axis=1))
        made = (mixed[:, :HEAD] / mixed[:, HEAD:]).astype(jnp.bfloat16)
        outs[:, :, here, :] = made.reshape(ROW, 2, UNIT, HEAD)


def time_attention(info, turned, values, out, turn, part, done):
    first, number = turn
    at, each_core = part
    units = min(each_core, ALONE // 2)
    rows = units * UNIT
    wide = pl.BlockSpec((ROW, 4, rows, HEAD), lambda h, i: (0, 0, i, first + h))
    thin = pl.BlockSpec((ROW, 2, rows, HEAD), lambda h, i: (0, 0, done // units + i, h))
    made = pl.BlockSpec((ROW, 2, rows, HEAD), lambda h, i: (0, 0, i, first + h))
    return pl.pallas_call(
        partial(time_kernel, at, each_core),
        grid=(number, each_core // units),
        in_specs=[SMEM, wide, thin] + ([] if out is None else [ANYWHERE]),
        out_specs=made,
        out_shape=half(ROW, 2, each_core * UNIT, PER * HEAD),
        input_output_aliases={} if out is None else {3: 0},
        compiler_params=params(),
        cost_estimate=cost(number * each_core * 16 * 16 * 256 * 128 * 4, number * 3, number * each_core * 65536),
        name="time",
    )(info, turned, values, *([] if out is None else [out]))


def divide_kernel(parts, info, pieces, own, *refs):
    gifts, (merged, in_sems, own_sem, gift_sems) = refs[:4], refs[4:]
    columns = pieces.shape[3]
    size = merged.shape[1] // UNIT
    begin = parts[0][0]
    start = info[START] + begin
    copies = []
    for place in range(ROW):
        chip, core = chip_and_core(place)
        done = 0
        for index, (at, each_core) in enumerate(parts):
            rows = each_core * UNIT
            to = pl.ds((at - begin) * UNIT + core * rows, rows)
            part = merged.at[:, to, pl.ds(chip * columns, columns)]
            copies.append(
                pltpu.make_async_copy(pieces.at[place, :, pl.ds(done, rows)], part, in_sems.at[place, index])
            )
            done += rows
    all_of(copies)
    copy = pltpu.make_async_copy(merged, own, own_sem)
    copy.start()

    def each(act):
        for way in range(4):
            for block in range(MOST):
                at = info[TAKEN_AT + way] + block - start

                @pl.when((block < info[TAKEN + way]) & (at >= 0) & (at < size))
                def _():
                    part = merged.at[:, pl.ds(lines(at), UNIT)]
                    to = gifts[way].at[:, pl.ds(block * UNIT, UNIT)]
                    act(pltpu.make_async_copy(part, to, gift_sems.at[way, block]))

    each(lambda copy: copy.start())
    each(lambda copy: copy.wait())
    copy.wait()


def divide(info, pieces, parts):
    features = CHIPS * pieces.shape[3]
    size = 2 * sum(each for _, each in parts)
    own, *gifts = pl.pallas_call(
        partial(divide_kernel, parts),
        in_specs=[SMEM, ANYWHERE],
        out_specs=[ANYWHERE] * 5,
        out_shape=[half(2, size * UNIT, features)] + [half(2, SPARE, features)] * 4,
        scratch_shapes=[
            pltpu.VMEM((2, size * UNIT, features), jnp.bfloat16),
            pltpu.SemaphoreType.DMA((ROW, 2)),
            pltpu.SemaphoreType.DMA,
            pltpu.SemaphoreType.DMA((4, MOST)),
        ],
        compiler_params=params(),
        cost_estimate=cost(0, max(1, 8 * features // FEATURES)),
        name="divide",
    )(info, pieces)
    return own, gifts


SPREAD = 64
SOURCE = 80


def unpack_kernel(adding, info, own, *refs):
    gifts, (other, out, held, made, own_sems, gift_sems, out_sems) = refs[:4], refs[4:]
    me, width, height = info[ME], info[WIDTH], info[HEIGHT]
    kept = info[KEPT]
    size = own.shape[1] // UNIT
    start = info[START] if adding else ALONE
    if adding:
        all_of([pltpu.make_async_copy(other, made, own_sems.at[0])])
        held[...] = jnp.zeros(held.shape, jnp.bfloat16)
    else:
        end = ALONE + size
        copies = [pltpu.make_async_copy(own, held.at[:, pl.ds(ALONE * UNIT, size * UNIT)], own_sems.at[ROW])]
        for place in range(ROW):
            chip, core = chip_and_core(place)
            rows, columns = other.shape[2], other.shape[3]
            to = held.at[:, pl.ds(core * rows, rows), pl.ds(chip * columns, columns)]
            copies.append(pltpu.make_async_copy(other.at[place], to, own_sems.at[place]))
        for copy in copies:
            copy.start()
        held[:, end * UNIT :, :] = jnp.zeros((2, held.shape[1] - end * UNIT, FEATURES), jnp.bfloat16)
        for copy in copies:
            copy.wait()
        for block in range(ALONE, end):

            @pl.when(block >= kept)
            def _():
                held[:, pl.ds(block * UNIT, UNIT), :] = jnp.zeros((2, UNIT, FEATURES), jnp.bfloat16)

    def each(act):
        if adding:
            for block in range(size):

                @pl.when(start + block < kept)
                def _():
                    part = own.at[:, pl.ds(block * UNIT, UNIT)]
                    act(pltpu.make_async_copy(part, held.at[:, pl.ds(lines(start + block), UNIT)], own_sems.at[block]))

        for way in range(4):
            for block in range(MOST):
                at = info[HOST_AT + way] + block - start

                @pl.when((block < info[GIVEN + way]) & (at >= 0) & (at < size))
                def _():
                    part = gifts[way].at[:, pl.ds(block * UNIT, UNIT)]
                    to = held.at[:, pl.ds(lines(info[GIVEN_AT + way] + block), UNIT)]
                    act(pltpu.make_async_copy(part, to, gift_sems.at[way, block]))

    each(lambda copy: copy.start())
    each(lambda copy: copy.wait())
    copies = []
    for index in range(SLOTS // SPREAD):
        row = index * 2
        from_row = pl.multiple_of((row * width) & -16, 16)
        at = lax.broadcasted_iota(jnp.int32, (SPREAD, SOURCE), 0)
        line = row + (at >> 5)
        wanted = line * width + (at & 31) - from_row
        wanted = jnp.where(((at & 31) < width) & (line < height), wanted, -1)
        picked = lax.broadcasted_iota(jnp.int32, (SPREAD, SOURCE), 1) == wanted
        to = pl.ds(index * SPREAD, SPREAD)
        for frame in range(2):
            alive = me * 2 + frame < info[FRAMES]
            matrix = jnp.where(picked & alive, 1.0, 0.0).astype(jnp.bfloat16)
            value = dot(matrix, held[frame, pl.ds(from_row, SOURCE), :])
            if adding:
                value = value + made[frame, to, :].astype(jnp.float32)
            made[frame, to, :] = value.astype(jnp.bfloat16)
            copy = pltpu.make_async_copy(made.at[frame, to], out.at[frame, to], out_sems.at[frame, index])
            copy.start()
            copies.append(copy)
    for copy in copies:
        copy.wait()


def unpack(info, own, gifts, other, adding):
    return pl.pallas_call(
        partial(unpack_kernel, adding),
        in_specs=[SMEM] + [ANYWHERE] * 6,
        out_specs=ANYWHERE,
        out_shape=half(2, SLOTS, FEATURES),
        input_output_aliases={6: 0} if adding else {},
        scratch_shapes=[
            pltpu.VMEM((2, SLOTS + SPARE, FEATURES), jnp.bfloat16),
            pltpu.VMEM((2, SLOTS, FEATURES), jnp.bfloat16),
            pltpu.SemaphoreType.DMA((max(MORE, ROW + 1),)),
            pltpu.SemaphoreType.DMA((4, MOST)),
            pltpu.SemaphoreType.DMA((2, SLOTS // SPREAD)),
        ],
        compiler_params=params(),
        cost_estimate=cost(0, 16),
        name="unpack",
    )(info, own, *gifts, other)


def step_along(value, way):
    size = lax.axis_size(AXES)
    return lax.ppermute(value, AXES, [(i, neighbour(i // ROW, way) * ROW + i % ROW) for i in range(size)])


def give(gifts):
    return [step_along(gifts[way], way) for way in range(4)]


def give_back(gifts):
    return [step_along(gifts[way], way ^ 1) for way in range(4)]


def exchange(pieces):
    size = lax.axis_size(AXES)
    groups = [list(range(i, i + ROW)) for i in range(0, size, ROW)]
    return lax.all_to_all(pieces, AXES, 0, 0, axis_index_groups=groups, tiled=True)


def after(value, *others):
    return lax.optimization_barrier((value, *others))[0]


def local(query_space, key_space, value_space, query_time, key_time, frame_counts, heights, widths):
    place = lax.axis_index(AXES).astype(jnp.int32).reshape(1)
    info, passes = make_plan(place, frame_counts, heights, widths)
    own, alone, gifts = pack(info, query_time, key_time)
    head = exchange(alone)
    gifts = give(gifts)
    spaced = []
    merged = []
    late = after(info, own)
    for index, turn in enumerate(TURNS):
        made, sent = space(late, query_space, key_space, value_space, turn)
        sent = give(sent)
        spaced.append((made, sent))
        if index == 0:
            pieces = merge(info, own, after(gifts, made), MAIN[1:])
            tail = exchange(after(pieces, head))
            sent = after(sent, pieces)
        merged.append(merge(info, made, sent, MAIN))
        late = after(info, pieces, merged[-1])
    previous = tail
    values = []
    for pieces in merged:
        previous = exchange(after(pieces, previous, spaced[-1][0]))
        values.append(previous)
    made_head = made_tail = None
    for turn, value in zip(TURNS, values):
        made_tail = time_attention(info, tail, value, made_tail, turn, MAIN[1], ALONE // 2)
        if turn is TURNS[-1]:
            back_tail = exchange(made_tail)
        made_head = time_attention(info, head, value, made_head, turn, MAIN[0], 0)
    back_head = exchange(after(made_head, back_tail))
    mine, back = divide(info, back_tail, MAIN[1:])
    out = unpack(info, mine, give_back(back), back_head, False)

    def further(index, out):
        here = info.at[START].set(ALONE + REST + index * MORE)
        turned = exchange(merge(here, own, gifts, FURTHER))
        made = None
        for (space_made, sent), turn in zip(spaced, TURNS):
            value = exchange(merge(here, space_made, sent, FURTHER))
            made = time_attention(here, turned, value, made, turn, FURTHER[0], 0)
        mine, back = divide(here, exchange(made), FURTHER)
        return unpack(here, mine, give_back(back), out, True)

    return lax.fori_loop(0, passes[0], further, out)


def solution(mesh):
    split = P(AXES, None, None)
    return jax.shard_map(
        local,
        mesh=mesh,
        in_specs=(split,) * 5 + (P(),) * 3,
        out_specs=split,
        check_vma=False,
    )
```

```python
from functools import partial

import jax
import jax.numpy as jnp
from jax import lax
from jax.experimental import pallas as pl
from jax.experimental.pallas import tpu as pltpu
from jax.sharding import PartitionSpec as P

HEAD = 128
WMAX = 32
HMAX = 22
ROW = 8
CHIPS = 4
PER = 3
SIDE = 4
ROWS = SIDE * SIDE
AXES = ("clip", "seq")
SLOTS = HMAX * WMAX
FEATURES = CHIPS * PER * HEAD
GAIN = HEAD**-0.5 * 1.4426950408889634
LOW = -1e30
UNIT = 16
BLOCKS = SLOTS // UNIT
MOST = 5
SPARE = MOST * UNIT
DIVISORS = (4, 2, 2)
ALONE = 10
REST = 20
MORE = 8
MAIN = ((0, ALONE // 2), (ALONE, REST // 2))
FURTHER = ((0, MORE // 2),)
TURNS = ((0, 1), (1, 2))
PACK = 64
REACH = 160
VMEM_LIMIT = 56 * 1024 * 1024

ME, WIDTH, COUNT, FRAMES, HEIGHT, KEPT, START = range(7)
GIVEN, GIVEN_AT, TAKEN, TAKEN_AT, HOST_AT = 8, 12, 16, 20, 24
FRAMES_OF = 32
TABLE = 128

SMEM = pl.BlockSpec(memory_space=pltpu.SMEM)
ANYWHERE = pl.BlockSpec(memory_space=pl.ANY)


def params():
    return pltpu.CompilerParams(vmem_limit_bytes=VMEM_LIMIT)


def cost(flops, megabytes, transcendentals=0):
    return pl.CostEstimate(flops=flops, bytes_accessed=megabytes * 2**20, transcendentals=transcendentals)


def half(*shape):
    return jax.ShapeDtypeStruct(shape, jnp.bfloat16)


def dot(left, right, transposed=False):
    dims = (((1,), (1 if transposed else 0,)), ((), ()))
    return lax.dot_general(left, right, dims, preferred_element_type=jnp.float32)


def lines(block):
    return pl.multiple_of(block * UNIT, UNIT)


def neighbour(row, way):
    z, y = row // SIDE, row % SIDE
    step = 1 if way % 2 == 0 else SIDE - 1
    if way < 2:
        return (z + step) % SIDE * SIDE + y
    return z * SIDE + (y + step) % SIDE


def plan_kernel(place, counts, heights, widths, table, passes, load, flow):
    me, mine = place[0] % ROW, place[0] // ROW

    def blocks(row):
        return (heights[row] * widths[row] + UNIT - 1) // UNIT

    for row in range(ROWS):
        load[row] = blocks(row)
        flow[0, row] = 0
        flow[1, row] = 0
    for divisor in DIVISORS:
        for axis in range(2):
            for row in range(ROWS):
                other = neighbour(row, 2 * axis)
                gap = load[row] - load[other]
                share = jnp.where(gap > 0, 1, -1) * lax.div(jnp.abs(gap), divisor)
                old = flow[axis, row]
                new = jnp.clip(old + share, -MOST, MOST)
                flow[axis, row] = new
                load[row] = load[row] - (new - old)
                load[other] = load[other] + (new - old)

    def edges_of(row):
        return [
            flow[0, row],
            -flow[0, neighbour(row, 1)],
            flow[1, row],
            -flow[1, neighbour(row, 3)],
        ]

    least = jnp.int32(BLOCKS)
    for row in range(ROWS):
        least = jnp.minimum(least, blocks(row) - sum(jnp.maximum(edge, 0) for edge in edges_of(row)))

    @pl.when(least < ALONE)
    def _():
        for row in range(ROWS):
            load[row] = blocks(row)
            flow[0, row] = 0
            flow[1, row] = 0

    largest = jnp.int32(0)
    for row in range(ROWS):
        largest = jnp.maximum(largest, load[row])
    passes[0] = jnp.maximum(largest - ALONE - REST + MORE - 1, 0) // MORE

    def list_of(row):
        edges = edges_of(row)
        kept = blocks(row) - sum(jnp.maximum(edge, 0) for edge in edges)
        given = [jnp.maximum(edges[way], 0) for way in range(4)]
        taken = [jnp.maximum(-edges[way ^ 1], 0) for way in range(4)]
        given_at, taken_at = [kept], [kept]
        for way in range(3):
            given_at.append(given_at[way] + given[way])
            taken_at.append(taken_at[way] + taken[way])
        return kept, given, given_at, taken, taken_at

    kept, given, given_at, taken, taken_at = list_of(mine)
    table[ME] = me
    table[WIDTH] = widths[mine]
    table[COUNT] = heights[mine] * widths[mine]
    table[FRAMES] = counts[mine]
    table[HEIGHT] = heights[mine]
    table[KEPT] = kept
    table[START] = 0
    for way in range(4):
        table[GIVEN + way] = given[way]
        table[GIVEN_AT + way] = given_at[way]
        table[TAKEN + way] = taken[way]
        table[TAKEN_AT + way] = taken_at[way]
        table[HOST_AT + way] = list_of(neighbour(mine, way))[4][way]

    def fill(slot, carry):
        table[FRAMES_OF + slot] = counts[mine]
        return carry

    lax.fori_loop(0, BLOCKS + MOST, fill, 0)
    for way in range(4):
        giver = neighbour(mine, way ^ 1)

        def mark(slot, carry):
            table[FRAMES_OF + slot] = counts[giver]
            return carry

        lax.fori_loop(taken_at[way], taken_at[way] + taken[way], mark, 0)


def make_plan(place, counts, heights, widths):
    return pl.pallas_call(
        plan_kernel,
        in_specs=[SMEM] * 4,
        out_specs=[SMEM] * 2,
        out_shape=[jax.ShapeDtypeStruct((TABLE,), jnp.int32), jax.ShapeDtypeStruct((1,), jnp.int32)],
        scratch_shapes=[pltpu.SMEM((ROWS,), jnp.int32), pltpu.SMEM((2, ROWS), jnp.int32)],
        cost_estimate=cost(1000, 0),
        name="plan",
    )(place, counts, heights, widths)


def gather_matrix(start, width, count):
    row = lax.div(start, width)
    base = jnp.minimum(row * WMAX, SLOTS - REACH)
    at = start + lax.broadcasted_iota(jnp.int32, (PACK, REACH), 0)
    line = jnp.full((PACK, REACH), row, jnp.int32)
    for step in range(1, 5):
        line = line + jnp.where(at >= (row + step) * width, 1, 0)
    slot = at + line * (WMAX - width) - base
    slot = jnp.where(at < count, slot, -1)
    picked = lax.broadcasted_iota(jnp.int32, (PACK, REACH), 1) == slot
    return jnp.where(picked, 1.0, 0.0).astype(jnp.bfloat16)


def reach_of(start, width):
    return pl.multiple_of(jnp.minimum(lax.div(start, width) * WMAX, SLOTS - REACH), WMAX)


def chip_and_core(place):
    return (place >> 2) * 2 + (place & 1), (place >> 1) & 1


def all_of(copies):
    for copy in copies:
        copy.start()
    for copy in copies:
        copy.wait()


def pack_kernel(info, queries, keys, own, alone, *refs):
    gifts, (picks, loaded, packed, in_sems, own_sems, alone_sems, gift_sems) = refs[:4], refs[4:]
    width, count = info[WIDTH], info[COUNT]
    loads = [
        pltpu.make_async_copy((queries, keys)[i // 2].at[i % 2], loaded.at[i], in_sems.at[i]) for i in range(4)
    ]
    for copy in loads:
        copy.start()
    for index in range(SLOTS // PACK):
        picks[index] = gather_matrix(index * PACK, width, count)
    packed[:, SLOTS:, :] = jnp.zeros((4, SPARE, FEATURES), jnp.bfloat16)
    copies = []
    rows = ALONE * UNIT // 2
    for i in range(4):
        loads[i].wait()
        for index in range(SLOTS // PACK):
            window = loaded[i, pl.ds(reach_of(index * PACK, width), REACH), :]
            packed[i, pl.ds(index * PACK, PACK), :] = dot(picks[index], window).astype(jnp.bfloat16)
        mine = [pltpu.make_async_copy(packed.at[i], own.at[i], own_sems.at[i])]
        for way in range(4):
            part = packed.at[i, pl.ds(lines(info[GIVEN_AT + way]), SPARE)]
            mine.append(pltpu.make_async_copy(part, gifts[way].at[i], gift_sems.at[i, way]))
        for place in range(ROW):
            chip, core = chip_and_core(place)
            part = packed.at[i, pl.ds(core * rows, rows), pl.ds(chip * PER * HEAD, PER * HEAD)]
            mine.append(pltpu.make_async_copy(part, alone.at[place, i], alone_sems.at[i, place]))
        for copy in mine:
            copy.start()
        copies += mine
    for copy in copies:
        copy.wait()


def pack(info, queries, keys):
    own, alone, *gifts = pl.pallas_call(
        pack_kernel,
        in_specs=[SMEM, ANYWHERE, ANYWHERE],
        out_specs=[ANYWHERE] * 6,
        out_shape=[half(4, SLOTS + SPARE, FEATURES), half(ROW, 4, ALONE * UNIT // 2, PER * HEAD)]
        + [half(4, SPARE, FEATURES)] * 4,
        scratch_shapes=[
            pltpu.VMEM((SLOTS // PACK, PACK, REACH), jnp.bfloat16),
            pltpu.VMEM((4, SLOTS, FEATURES), jnp.bfloat16),
            pltpu.VMEM((4, SLOTS + SPARE, FEATURES), jnp.bfloat16),
            pltpu.SemaphoreType.DMA((4,)),
            pltpu.SemaphoreType.DMA((4,)),
            pltpu.SemaphoreType.DMA((4, ROW)),
            pltpu.SemaphoreType.DMA((4, 4)),
        ],
        compiler_params=params(),
        cost_estimate=cost(0, 40),
        name="pack",
    )(info, queries, keys)
    return own, alone, gifts


def merge_kernel(parts, info, own, *refs):
    gifts, (out, merged, own_sem, gift_sems, out_sems) = refs[:4], refs[4:]
    columns = out.shape[3]
    first = parts[0][0]
    start = info[START] + first
    size = merged.shape[1] // UNIT
    copy = pltpu.make_async_copy(own.at[:, pl.ds(lines(start), size * UNIT)], merged, own_sem)
    copy.start()
    copy.wait()

    def each(act):
        for way in range(4):
            for block in range(MOST):
                at = info[TAKEN_AT + way] + block - start

                @pl.when((block < info[TAKEN + way]) & (at >= 0) & (at < size))
                def _():
                    part = gifts[way].at[:, pl.ds(block * UNIT, UNIT)]
                    to = merged.at[:, pl.ds(lines(at), UNIT)]
                    act(pltpu.make_async_copy(part, to, gift_sems.at[way, block]))

    each(lambda copy: copy.start())
    each(lambda copy: copy.wait())
    copies = []
    for place in range(ROW):
        chip, core = chip_and_core(place)
        done = 0
        for index, (at, each_core) in enumerate(parts):
            rows = each_core * UNIT
            part = merged.at[:, pl.ds((at - first) * UNIT + core * rows, rows), pl.ds(chip * columns, columns)]
            to = out.at[place, :, pl.ds(done, rows)]
            copies.append(pltpu.make_async_copy(part, to, out_sems.at[place, index]))
            done += rows
    all_of(copies)


def merge(info, own, gifts, parts):
    count, _, features = own.shape
    rows = sum(each for _, each in parts) * UNIT
    return pl.pallas_call(
        partial(merge_kernel, parts),
        in_specs=[SMEM] + [ANYWHERE] * 5,
        out_specs=ANYWHERE,
        out_shape=half(ROW, count, rows, features // CHIPS),
        scratch_shapes=[
            pltpu.VMEM((count, 2 * rows, features), jnp.bfloat16),
            pltpu.SemaphoreType.DMA,
            pltpu.SemaphoreType.DMA((4, MOST)),
            pltpu.SemaphoreType.DMA((ROW, 2)),
        ],
        compiler_params=params(),
        cost_estimate=cost(0, max(1, 6 * count * features // FEATURES)),
        name="merge",
    )(info, own, *gifts)


QBLOCK = SLOTS // 2


def space_kernel(number, info, q_ref, k_ref, v_ref, own, *refs):
    gifts, (picks, qc, kc, vc, made, own_sem, gift_sems) = refs[:4], refs[4:]
    frame, which = pl.program_id(0), pl.program_id(1)
    me, width, count = info[ME], info[WIDTH], info[COUNT]
    alive = me * 2 + frame < info[FRAMES]
    column = pl.ds(pl.multiple_of(which * HEAD, HEAD), HEAD)

    @pl.when((frame == 0) & (which == 0))
    def _():
        vc[:, HEAD:] = jnp.ones((SLOTS, HEAD), jnp.bfloat16)
        made[:, SLOTS:, :] = jnp.zeros((2, SPARE, CHIPS * number * HEAD), jnp.bfloat16)
        for index in range(SLOTS // PACK):
            picks[index] = gather_matrix(index * PACK, width, count)

    @pl.when(alive)
    def _():
        for index in range(SLOTS // PACK):
            at = pl.ds(reach_of(index * PACK, width), REACH)
            to = pl.ds(index * PACK, PACK)
            window = jnp.concatenate([q_ref[0, at, :], k_ref[0, at, :], v_ref[0, at, :]], axis=1)
            found = dot(picks[index], window).astype(jnp.bfloat16)
            qc[to, :] = found[:, :HEAD]
            kc[to, :] = found[:, HEAD : 2 * HEAD]
            vc[to, :HEAD] = found[:, 2 * HEAD :]

    bias = jnp.where(lax.broadcasted_iota(jnp.int32, (1, SLOTS), 1) < count, 0.0, LOW)

    def attend(block):
        to = pl.ds(block * QBLOCK, QBLOCK)
        scores = dot(qc[to, :], kc[...], True) + bias
        top = jnp.max(scores, axis=-1, keepdims=True)
        expo = jnp.exp2((scores - top) * GAIN).astype(jnp.bfloat16)
        mixed = dot(expo, vc[...])
        made[frame, to, column] = (mixed[:, :HEAD] / mixed[:, HEAD:]).astype(jnp.bfloat16)

    def blank(block):
        made[frame, pl.ds(block * QBLOCK, QBLOCK), column] = jnp.zeros((QBLOCK, HEAD), jnp.bfloat16)

    @pl.when(alive & (count > QBLOCK))
    def _():
        attend(0)
        attend(1)

    @pl.when(alive & (count <= QBLOCK))
    def _():
        attend(0)
        blank(1)

    @pl.when(jnp.logical_not(alive))
    def _():
        blank(0)
        blank(1)

    @pl.when((frame == 1) & (which == CHIPS * number - 1))
    def _():
        copies = [pltpu.make_async_copy(made, own, own_sem)]
        for way in range(4):
            part = made.at[:, pl.ds(lines(info[GIVEN_AT + way]), SPARE)]
            copies.append(pltpu.make_async_copy(part, gifts[way], gift_sems.at[way]))
        all_of(copies)


def space(info, queries, keys, values, turn):
    first, number = turn
    features = CHIPS * number * HEAD
    spec = pl.BlockSpec((1, SLOTS, HEAD), lambda f, i: (f, 0, i // number * PER + first + i % number))
    steps = 2 * CHIPS * number
    own, *gifts = pl.pallas_call(
        partial(space_kernel, number),
        grid=(2, CHIPS * number),
        in_specs=[SMEM, spec, spec, spec],
        out_specs=[ANYWHERE] * 5,
        out_shape=[half(2, SLOTS + SPARE, features)] + [half(2, SPARE, features)] * 4,
        scratch_shapes=[
            pltpu.VMEM((SLOTS // PACK, PACK, REACH), jnp.bfloat16),
            pltpu.VMEM((SLOTS, HEAD), jnp.bfloat16),
            pltpu.VMEM((SLOTS, HEAD), jnp.bfloat16),
            pltpu.VMEM((SLOTS, 2 * HEAD), jnp.bfloat16),
            pltpu.VMEM((2, SLOTS + SPARE, features), jnp.bfloat16),
            pltpu.SemaphoreType.DMA,
            pltpu.SemaphoreType.DMA((4,)),
        ],
        compiler_params=params(),
        cost_estimate=cost(steps * 8 * SLOTS * SLOTS * HEAD, number * 8, steps * SLOTS * SLOTS),
        name="space",
    )(info, queries, keys, values)
    return own, gifts


def time_kernel(at, each_core, info, turned, vs, *refs):
    outs = refs[-1]
    rows = outs.shape[2]
    core = (info[ME] >> 1) & 1
    first = info[START] + at + core * each_core + pl.program_id(1) * (rows // UNIT)
    span = ROW * 2 * UNIT
    down = lax.broadcasted_iota(jnp.int32, (span, span), 0)
    along = lax.broadcasted_iota(jnp.int32, (span, span), 1)
    frame = jnp.where((down & 15) == (along & 15), along >> 4, span)
    ones = jnp.ones((span, HEAD), jnp.bfloat16)
    for index in range(rows // UNIT):
        here = pl.ds(index * UNIT, UNIT)
        seen = frame < info[FRAMES_OF + first + index]
        queries = turned[:, 0:2, here, :].reshape(span, HEAD)
        keys = turned[:, 2:4, here, :].reshape(span, HEAD)
        values = vs[:, :, here, :].reshape(span, HEAD)
        scores = jnp.where(seen, dot(queries, keys, True), LOW)
        top = jnp.max(scores, axis=-1, keepdims=True)
        expo = jnp.exp2((scores - top) * GAIN).astype(jnp.bfloat16)
        mixed = dot(expo, jnp.concatenate([values, ones], axis=1))
        made = (mixed[:, :HEAD] / mixed[:, HEAD:]).astype(jnp.bfloat16)
        outs[:, :, here, :] = made.reshape(ROW, 2, UNIT, HEAD)


def time_attention(info, turned, values, out, turn, part, done):
    first, number = turn
    at, each_core = part
    units = min(each_core, ALONE // 2)
    rows = units * UNIT
    wide = pl.BlockSpec((ROW, 4, rows, HEAD), lambda h, i: (0, 0, i, first + h))
    thin = pl.BlockSpec((ROW, 2, rows, HEAD), lambda h, i: (0, 0, done // units + i, h))
    made = pl.BlockSpec((ROW, 2, rows, HEAD), lambda h, i: (0, 0, i, first + h))
    return pl.pallas_call(
        partial(time_kernel, at, each_core),
        grid=(number, each_core // units),
        in_specs=[SMEM, wide, thin] + ([] if out is None else [ANYWHERE]),
        out_specs=made,
        out_shape=half(ROW, 2, each_core * UNIT, PER * HEAD),
        input_output_aliases={} if out is None else {3: 0},
        compiler_params=params(),
        cost_estimate=cost(number * each_core * 16 * 16 * 256 * 128 * 4, number * 3, number * each_core * 65536),
        name="time",
    )(info, turned, values, *([] if out is None else [out]))


def divide_kernel(parts, info, pieces, own, *refs):
    gifts, (merged, in_sems, own_sem, gift_sems) = refs[:4], refs[4:]
    columns = pieces.shape[3]
    size = merged.shape[1] // UNIT
    begin = parts[0][0]
    start = info[START] + begin
    copies = []
    for place in range(ROW):
        chip, core = chip_and_core(place)
        done = 0
        for index, (at, each_core) in enumerate(parts):
            rows = each_core * UNIT
            to = pl.ds((at - begin) * UNIT + core * rows, rows)
            part = merged.at[:, to, pl.ds(chip * columns, columns)]
            copies.append(
                pltpu.make_async_copy(pieces.at[place, :, pl.ds(done, rows)], part, in_sems.at[place, index])
            )
            done += rows
    all_of(copies)
    copy = pltpu.make_async_copy(merged, own, own_sem)
    copy.start()

    def each(act):
        for way in range(4):
            for block in range(MOST):
                at = info[TAKEN_AT + way] + block - start

                @pl.when((block < info[TAKEN + way]) & (at >= 0) & (at < size))
                def _():
                    part = merged.at[:, pl.ds(lines(at), UNIT)]
                    to = gifts[way].at[:, pl.ds(block * UNIT, UNIT)]
                    act(pltpu.make_async_copy(part, to, gift_sems.at[way, block]))

    each(lambda copy: copy.start())
    each(lambda copy: copy.wait())
    copy.wait()


def divide(info, pieces, parts):
    features = CHIPS * pieces.shape[3]
    size = 2 * sum(each for _, each in parts)
    own, *gifts = pl.pallas_call(
        partial(divide_kernel, parts),
        in_specs=[SMEM, ANYWHERE],
        out_specs=[ANYWHERE] * 5,
        out_shape=[half(2, size * UNIT, features)] + [half(2, SPARE, features)] * 4,
        scratch_shapes=[
            pltpu.VMEM((2, size * UNIT, features), jnp.bfloat16),
            pltpu.SemaphoreType.DMA((ROW, 2)),
            pltpu.SemaphoreType.DMA,
            pltpu.SemaphoreType.DMA((4, MOST)),
        ],
        compiler_params=params(),
        cost_estimate=cost(0, max(1, 8 * features // FEATURES)),
        name="divide",
    )(info, pieces)
    return own, gifts


SPREAD = 64
SOURCE = 80


def unpack_kernel(adding, info, own, *refs):
    gifts, (other, out, held, made, own_sems, gift_sems, out_sems) = refs[:4], refs[4:]
    me, width, height = info[ME], info[WIDTH], info[HEIGHT]
    kept = info[KEPT]
    size = own.shape[1] // UNIT
    start = info[START] if adding else ALONE
    if adding:
        all_of([pltpu.make_async_copy(other, made, own_sems.at[0])])
        held[...] = jnp.zeros(held.shape, jnp.bfloat16)
    else:
        end = ALONE + size
        copies = [pltpu.make_async_copy(own, held.at[:, pl.ds(ALONE * UNIT, size * UNIT)], own_sems.at[ROW])]
        for place in range(ROW):
            chip, core = chip_and_core(place)
            rows, columns = other.shape[2], other.shape[3]
            to = held.at[:, pl.ds(core * rows, rows), pl.ds(chip * columns, columns)]
            copies.append(pltpu.make_async_copy(other.at[place], to, own_sems.at[place]))
        for copy in copies:
            copy.start()
        held[:, end * UNIT :, :] = jnp.zeros((2, held.shape[1] - end * UNIT, FEATURES), jnp.bfloat16)
        for copy in copies:
            copy.wait()
        for block in range(ALONE, end):

            @pl.when(block >= kept)
            def _():
                held[:, pl.ds(block * UNIT, UNIT), :] = jnp.zeros((2, UNIT, FEATURES), jnp.bfloat16)

    def each(act):
        if adding:
            for block in range(size):

                @pl.when(start + block < kept)
                def _():
                    part = own.at[:, pl.ds(block * UNIT, UNIT)]
                    act(pltpu.make_async_copy(part, held.at[:, pl.ds(lines(start + block), UNIT)], own_sems.at[block]))

        for way in range(4):
            for block in range(MOST):
                at = info[HOST_AT + way] + block - start

                @pl.when((block < info[GIVEN + way]) & (at >= 0) & (at < size))
                def _():
                    part = gifts[way].at[:, pl.ds(block * UNIT, UNIT)]
                    to = held.at[:, pl.ds(lines(info[GIVEN_AT + way] + block), UNIT)]
                    act(pltpu.make_async_copy(part, to, gift_sems.at[way, block]))

    each(lambda copy: copy.start())
    each(lambda copy: copy.wait())
    copies = []
    for index in range(SLOTS // SPREAD):
        row = index * 2
        from_row = pl.multiple_of((row * width) & -16, 16)
        at = lax.broadcasted_iota(jnp.int32, (SPREAD, SOURCE), 0)
        line = row + (at >> 5)
        wanted = line * width + (at & 31) - from_row
        wanted = jnp.where(((at & 31) < width) & (line < height), wanted, -1)
        picked = lax.broadcasted_iota(jnp.int32, (SPREAD, SOURCE), 1) == wanted
        to = pl.ds(index * SPREAD, SPREAD)
        for frame in range(2):
            alive = me * 2 + frame < info[FRAMES]
            matrix = jnp.where(picked & alive, 1.0, 0.0).astype(jnp.bfloat16)
            value = dot(matrix, held[frame, pl.ds(from_row, SOURCE), :])
            if adding:
                value = value + made[frame, to, :].astype(jnp.float32)
            made[frame, to, :] = value.astype(jnp.bfloat16)
            copy = pltpu.make_async_copy(made.at[frame, to], out.at[frame, to], out_sems.at[frame, index])
            copy.start()
            copies.append(copy)
    for copy in copies:
        copy.wait()


def unpack(info, own, gifts, other, adding):
    return pl.pallas_call(
        partial(unpack_kernel, adding),
        in_specs=[SMEM] + [ANYWHERE] * 6,
        out_specs=ANYWHERE,
        out_shape=half(2, SLOTS, FEATURES),
        input_output_aliases={6: 0} if adding else {},
        scratch_shapes=[
            pltpu.VMEM((2, SLOTS + SPARE, FEATURES), jnp.bfloat16),
            pltpu.VMEM((2, SLOTS, FEATURES), jnp.bfloat16),
            pltpu.SemaphoreType.DMA((max(MORE, ROW + 1),)),
            pltpu.SemaphoreType.DMA((4, MOST)),
            pltpu.SemaphoreType.DMA((2, SLOTS // SPREAD)),
        ],
        compiler_params=params(),
        cost_estimate=cost(0, 16),
        name="unpack",
    )(info, own, *gifts, other)


def step_along(value, way):
    size = lax.axis_size(AXES)
    return lax.ppermute(value, AXES, [(i, neighbour(i // ROW, way) * ROW + i % ROW) for i in range(size)])


def give(gifts):
    return [step_along(gifts[way], way) for way in range(4)]


def give_back(gifts):
    return [step_along(gifts[way], way ^ 1) for way in range(4)]


def exchange(pieces):
    size = lax.axis_size(AXES)
    groups = [list(range(i, i + ROW)) for i in range(0, size, ROW)]
    return lax.all_to_all(pieces, AXES, 0, 0, axis_index_groups=groups, tiled=True)


def after(value, *others):
    return lax.optimization_barrier((value, *others))[0]


def local(query_space, key_space, value_space, query_time, key_time, frame_counts, heights, widths):
    place = lax.axis_index(AXES).astype(jnp.int32).reshape(1)
    info, passes = make_plan(place, frame_counts, heights, widths)
    own, alone, gifts = pack(info, query_time, key_time)
    head = exchange(alone)
    gifts = give(gifts)
    spaced = []
    merged = []
    late = after(info, own)
    for index, turn in enumerate(TURNS):
        made, sent = space(late, query_space, key_space, value_space, turn)
        sent = give(sent)
        spaced.append((made, sent))
        if index == 0:
            pieces = merge(info, own, after(gifts, made), MAIN[1:])
            tail = exchange(after(pieces, head))
            sent = after(sent, pieces)
        merged.append(merge(info, made, sent, MAIN))
        late = after(info, pieces, merged[-1])
    previous = tail
    values = []
    for pieces in merged:
        previous = exchange(after(pieces, previous, spaced[-1][0]))
        values.append(previous)
    made_head = made_tail = None
    for turn, value in zip(TURNS, values):
        made_tail = time_attention(info, tail, value, made_tail, turn, MAIN[1], ALONE // 2)
        if turn is TURNS[-1]:
            back_tail = exchange(made_tail)
        made_head = time_attention(info, head, value, made_head, turn, MAIN[0], 0)
    back_head = exchange(after(made_head, back_tail))
    mine, back = divide(info, back_tail, MAIN[1:])
    out = unpack(info, mine, give_back(back), back_head, False)

    def further(index, out):
        here = info.at[START].set(ALONE + REST + index * MORE)
        turned = exchange(merge(here, own, gifts, FURTHER))
        made = None
        for (space_made, sent), turn in zip(spaced, TURNS):
            value = exchange(merge(here, space_made, sent, FURTHER))
            made = time_attention(here, turned, value, made, turn, FURTHER[0], 0)
        mine, back = divide(here, exchange(made), FURTHER)
        return unpack(here, mine, give_back(back), out, True)

    return lax.fori_loop(0, passes[0], further, out)


def solution(mesh):
    split = P(AXES, None, None)
    return jax.shard_map(
        local,
        mesh=mesh,
        in_specs=(split,) * 5 + (P(),) * 3,
        out_specs=split,
        check_vma=False,
    )
```
